32 devices in a mesh: groups: 2 (over x), row: 16 (over z, y, core).
Axes of the slice: x: 2, y: 2, z: 4, core: 2. Of those that a mesh axis runs over, the one named last changes fastest.
Arguments:
- panels: float32 [53248, 768], P(('groups', 'row')), parts along dimension 0, as said below
- weights: float32 [53248, 1792], P(('groups', 'row')), parts along dimension 0, may hold values from -6 to 6
- block_ids: int32 [6], P('groups'), parts along dimension 0, may hold values from 0 to 103, as said below
Outputs:
- pruned_weights: float32 [53248, 1792], P(('groups', 'row')), parts along dimension 0
- losses: float32 [6], P('groups'), parts along dimension 0
The draws below stay inside these ranges and needn't reach their ends.
There are 2 independent parts, one for each index of `groups`. The reference program is written for one: setup_inputs(seed, part) draws one part's arguments, and reference() takes and returns one part's arrays. A program takes and returns all parts, laid end to end along the dimension named above; each array names one. Nothing has to cross between parts.
Inputs may be any that keep to these rules, and one draw needn't show every extreme that they name: `panels`: the columns, at the listed blocks' hidden units and in pick order, of a symmetric positive definite matrix of order 26624. `block_ids`: 3 distinct block numbers; the first and the last block of the window are always among them.
All inputs are finite; a program needn't handle non-finite values.
Results may differ from the reference program's by a relative error of at most 0.00017.
Values sent between devices are 32-bit elements; how exact they have to be, the bound alone decides.
A program may use at most 128 MiB of HBM per device.

```python
import jax
import jax.numpy as jnp
from jax import lax

ORDER = 26624
COLS = 1792
BLOCK = 256
PICKS = 3


def chosen_blocks(key):
    block_count = ORDER // BLOCK
    middle = 1 + jax.random.permutation(jax.random.fold_in(key, 7), block_count - 2)[:PICKS - 2]
    ends = jnp.array([0, block_count - 1], dtype=jnp.int32)
    listed = jnp.concatenate([ends, middle.astype(jnp.int32)])
    shuffle = jax.random.permutation(jax.random.fold_in(key, 13), PICKS)
    return listed[shuffle].astype(jnp.int32)


def draw_block_ids(key, part):
    return chosen_blocks(key)


def draw_panels(key, part):
    block_list = chosen_blocks(key)
    columns = (block_list[:, None] * BLOCK + jnp.arange(BLOCK, dtype=jnp.int32)[None, :]).reshape(-1)
    keys = jax.random.split(jax.random.fold_in(key, 11), 2)
    inner = 4 * BLOCK
    factors = jax.random.normal(keys[0], (ORDER, inner), jnp.float32)
    diagonal = jnp.exp(jax.random.uniform(keys[1], (ORDER,), jnp.float32, jnp.log(0.5), jnp.log(2.0)))
    picked = factors[columns]
    matrix = jnp.dot(factors, picked.T, precision=lax.Precision.HIGHEST) / inner
    all_rows = jnp.arange(ORDER, dtype=jnp.int32)
    matrix = matrix + jnp.where(all_rows[:, None] == columns[None, :], diagonal[:, None], 0.0)
    return matrix.astype(jnp.float32)


def levels(key, shape, cuts, low, high):
    factor_of, own = 1.0, jax.random.fold_in(key, 6)
    for position, shards_of in cuts:
        steps = jnp.exp(jax.random.uniform(jax.random.fold_in(own, position), (shards_of,), jnp.float32, low / len(cuts), high / len(cuts)))
        factor_of = factor_of * jnp.repeat(steps, shape[position] // shards_of).reshape([-1 if axis == position else 1 for axis in range(len(shape))])
    return factor_of


def normal_values(own_key, shape, scale, reach, cuts=(), kind=jnp.bfloat16):
    entries = jax.random.normal(own_key, shape, jnp.float32) * scale
    if len(cuts) > 0:
        entries = levels(own_key, shape, cuts, -0.22, 0.18) * entries
    return jnp.clip(entries, min=-reach, max=reach).astype(kind)


def setup_inputs(seed: int = 0, part: int = 0) -> dict:
    arg_keys = jax.random.split(jax.random.key(seed), 4)
    own_keys = jax.random.split(jax.random.fold_in(arg_keys[3], part), 4)
    return {
        "panels": draw_panels(jax.random.fold_in(jax.random.fold_in(arg_keys[3], part), 71), part),
        "weights": normal_values(own_keys[1], (ORDER, COLS), 1.0, 6.0, ((0, 16),), jnp.float32),
        "block_ids": draw_block_ids(jax.random.fold_in(jax.random.fold_in(arg_keys[3], part), 71), part),
    }


exact_mode = lax.Precision.HIGHEST

def chol_solve(factor, rhs):
    middle = lax.linalg.triangular_solve(factor, rhs, left_side=True, lower=True)
    return lax.linalg.triangular_solve(factor, middle, left_side=True, lower=True, transpose_a=True)

def reference(panels, weights, block_ids):
    current_panels = panels
    current = weights
    losses = []
    all_rows = jnp.arange(ORDER, dtype=jnp.int32)
    zero_index = jnp.zeros((), jnp.int32)
    for number in range(PICKS):
        start_row = (block_ids[number] * BLOCK).astype(jnp.int32)
        low_edge = number * BLOCK
        row_block = lax.dynamic_slice(current_panels, (start_row, zero_index), (BLOCK, PICKS * BLOCK))
        diag_block = row_block[:, low_edge:low_edge + BLOCK]
        col_panel = current_panels[:, low_edge:low_edge + BLOCK]
        chosen = lax.dynamic_slice(current, (start_row, zero_index), (BLOCK, COLS))
        factor = jnp.linalg.cholesky(diag_block)
        solved = chol_solve(factor, chosen)
        losses.append(jnp.sum(chosen * solved) / (2.0 * BLOCK * COLS))
        current = current - jnp.dot(col_panel, solved, precision=exact_mode)
        inside = (all_rows >= start_row) & (all_rows < start_row + BLOCK)
        current = jnp.where(inside[:, None], jnp.zeros_like(current), current)
        if number < PICKS - 1:
            left_factor = chol_solve(factor, col_panel.T).T
            current_panels = current_panels - jnp.dot(left_factor, row_block, precision=exact_mode)
    return (current, jnp.stack(losses))
```

```python
import jax
import jax.numpy as jnp
from jax import lax
from jax.experimental import pallas as pl
from jax.experimental.pallas import tpu as pltpu
from jax.sharding import PartitionSpec as P

BLOCK = 256
TILE = 128
exact_mode = lax.Precision.HIGHEST
split_mode = lax.Precision.HIGH


def dot_nt(a, b):
    return lax.dot_general(a, b, (((1,), (1,)), ((), ())), precision=exact_mode,
                           preferred_element_type=jnp.float32)


def dot_nn(a, b):
    return lax.dot_general(a, b, (((1,), (0,)), ((), ())), precision=exact_mode,
                           preferred_element_type=jnp.float32)


def factor_tile(tile):
    n = TILE
    groups = n // 8
    rows = lax.broadcasted_iota(jnp.int32, (8, n), 0)
    lanes = lax.broadcasted_iota(jnp.int32, (8, n), 1)
    left = [tile[8 * g : 8 * g + 8, :] for g in range(groups)]
    right = [jnp.where(lanes == rows + 8 * g, 1.0, 0.0) for g in range(groups)]
    done = []
    for j in range(0, n, 2):
        g, o = j // 8, j % 8
        c0 = {i: jnp.broadcast_to(left[i][:, j : j + 1], (8, n)) for i in range(g, groups)}
        c1 = {i: jnp.broadcast_to(left[i][:, j + 1 : j + 2], (8, n)) for i in range(g, groups)}
        a = c0[g][o : o + 1]
        b = c0[g][o + 1 : o + 2]
        d = c1[g][o + 1 : o + 2]
        inv_det = 1.0 / (a * d - b * b)
        m00, m01, m11 = d * inv_det, -b * inv_det, a * inv_det
        r0, r1 = left[g][o : o + 1], left[g][o + 1 : o + 2]
        s0, s1 = right[g][o : o + 1], right[g][o + 1 : o + 2]
        q0, q1 = m00 * r0 + m01 * r1, m01 * r0 + m11 * r1
        t0, t1 = m00 * s0 + m01 * s1, m01 * s0 + m11 * s1
        ratio = b / a
        done.append(s0 * lax.rsqrt(a))
        done.append((s1 - ratio * s0) * lax.rsqrt(d - b * ratio))
        for i in range(g, groups):
            k0, k1 = c0[i], c1[i]
            if i == g:
                if o == 6:
                    continue
                keep = rows > o + 1
                k0, k1 = jnp.where(keep, k0, 0.0), jnp.where(keep, k1, 0.0)
            left[i] = left[i] - (k0 * q0 + k1 * q1)
            right[i] = right[i] - (k0 * t0 + k1 * t1)
    return jnp.concatenate(done, axis=0)


def invert_kernel(c_ref, z_ref, m_ref, p_ref):
    n = c_ref.shape[0]
    m_ref[...] = c_ref[...]
    z_ref[...] = jnp.where(
        lax.broadcasted_iota(jnp.int32, (n, n), 0) == lax.broadcasted_iota(jnp.int32, (n, n), 1), 1.0, 0.0)

    def step(k, carry):
        here = pl.ds(pl.multiple_of(k * TILE, TILE), TILE)
        inv = factor_tile(m_ref[here, here])
        below = lax.broadcasted_iota(jnp.int32, (n, TILE), 0) >= (k + 1) * TILE
        p_ref[...] = jnp.where(below, dot_nt(m_ref[:, here], inv), 0.0)
        z_ref[here, :] = dot_nn(inv, z_ref[here, :])
        panel = p_ref[...]
        for part in range(0, n, BLOCK):
            cut = slice(part, part + BLOCK)
            m_ref[:, cut] = m_ref[:, cut] - dot_nt(panel, p_ref[cut, :])
            z_ref[:, cut] = z_ref[:, cut] - dot_nn(panel, z_ref[here, cut])
        return carry

    lax.fori_loop(0, n // TILE, step, 0)


def inverse_factor(cross):
    n = cross.shape[0]
    return pl.pallas_call(
        invert_kernel,
        out_shape=jax.ShapeDtypeStruct((n, n), jnp.float32),
        in_specs=[pl.BlockSpec(memory_space=pltpu.VMEM)],
        out_specs=pl.BlockSpec(memory_space=pltpu.VMEM),
        scratch_shapes=[pltpu.VMEM((n, n), jnp.float32), pltpu.VMEM((n, TILE), jnp.float32)],
        compiler_params=pltpu.CompilerParams(vmem_limit_bytes=32 * 1024 * 1024),
        cost_estimate=pl.CostEstimate(flops=40_000_000_000, bytes_accessed=8 * n * n, transcendentals=0),
    )(cross)


def own_rows(array, start):
    rows = array.shape[0]
    inside = jnp.clip(start, 0, rows - BLOCK)
    part = lax.dynamic_slice_in_dim(array, inside, BLOCK, 0)
    blank = jnp.zeros_like(part)
    shift = jnp.clip(start - inside, -BLOCK, BLOCK)
    return lax.dynamic_slice_in_dim(jnp.concatenate([blank, part, blank], axis=0), BLOCK + shift, BLOCK, 0)


def body(panels, weights, block_ids):
    local_rows = panels.shape[0]
    picks = block_ids.shape[0]
    cols = weights.shape[1]
    first_row = lax.axis_index("row") * local_rows
    starts = [block_ids[k] * BLOCK - first_row for k in range(picks)]

    pieces = []
    for k in range(picks):
        taken = own_rows(panels, starts[k])
        pieces += [taken[:, j * BLOCK : (j + 1) * BLOCK] for j in range(k + 1)]
    pieces = lax.psum(jnp.concatenate(pieces, axis=0), "row")
    listed = jnp.concatenate([own_rows(weights, starts[k]) for k in range(picks)], axis=0)
    pieces, listed = lax.optimization_barrier((pieces, listed))
    listed = lax.psum(listed, "row")

    def piece(i, j):
        if i < j:
            return piece(j, i).T
        at = (i * (i + 1) // 2 + j) * BLOCK
        return pieces[at : at + BLOCK]

    cross = jnp.concatenate(
        [jnp.concatenate([piece(i, j) for j in range(picks)], axis=1) for i in range(picks)], axis=0)
    inverse = inverse_factor(cross)
    left = lax.dot_general(panels, inverse, (((1,), (1,)), ((), ())), precision=split_mode)
    middle = jnp.dot(inverse, listed, precision=split_mode)
    losses = jnp.sum((middle * middle).reshape(picks, -1), axis=1) / (BLOCK * cols * 2.0)
    local = jnp.arange(local_rows, dtype=jnp.int32)
    keep = jnp.ones((local_rows,), jnp.bool_)
    for start in starts:
        keep = keep & ((local < start) | (local >= start + BLOCK))
    update = weights - jnp.dot(left, middle, precision=split_mode)
    return (jnp.where(keep[:, None], update, 0.0), losses)


def solution(mesh):
    in_specs = (P(("groups", "row"), None), P(("groups", "row"), None), P("groups"))
    out_specs = (P(("groups", "row"), None), P("groups"))
    return jax.shard_map(body, mesh=mesh, in_specs=in_specs, out_specs=out_specs, check_vma=False)
```

```python
import jax
import jax.numpy as jnp
from jax import lax
from jax.experimental import pallas as pl
from jax.experimental.pallas import tpu as pltpu
from jax.sharding import PartitionSpec as P

BLOCK = 256
TILE = 128
exact_mode = lax.Precision.HIGHEST
split_mode = lax.Precision.HIGH


def dot_nt(a, b):
    return lax.dot_general(a, b, (((1,), (1,)), ((), ())), precision=exact_mode,
                           preferred_element_type=jnp.float32)


def dot_nn(a, b):
    return lax.dot_general(a, b, (((1,), (0,)), ((), ())), precision=exact_mode,
                           preferred_element_type=jnp.float32)


def factor_tile(tile):
    n = TILE
    groups = n // 8
    rows = lax.broadcasted_iota(jnp.int32, (8, n), 0)
    lanes = lax.broadcasted_iota(jnp.int32, (8, n), 1)
    left = [tile[8 * g : 8 * g + 8, :] for g in range(groups)]
    right = [jnp.where(lanes == rows + 8 * g, 1.0, 0.0) for g in range(groups)]
    done = []
    for j in range(0, n, 2):
        g, o = j // 8, j % 8
        c0 = {i: jnp.broadcast_to(left[i][:, j : j + 1], (8, n)) for i in range(g, groups)}
        c1 = {i: jnp.broadcast_to(left[i][:, j + 1 : j + 2], (8, n)) for i in range(g, groups)}
        a = c0[g][o : o + 1]
        b = c0[g][o + 1 : o + 2]
        d = c1[g][o + 1 : o + 2]
        inv_det = 1.0 / (a * d - b * b)
        m00, m01, m11 = d * inv_det, -b * inv_det, a * inv_det
        r0, r1 = left[g][o : o + 1], left[g][o + 1 : o + 2]
        s0, s1 = right[g][o : o + 1], right[g][o + 1 : o + 2]
        q0, q1 = m00 * r0 + m01 * r1, m01 * r0 + m11 * r1
        t0, t1 = m00 * s0 + m01 * s1, m01 * s0 + m11 * s1
        ratio = b / a
        done.append(s0 * lax.rsqrt(a))
        done.append((s1 - ratio * s0) * lax.rsqrt(d - b * ratio))
        for i in range(g, groups):
            k0, k1 = c0[i], c1[i]
            if i == g:
                if o == 6:
                    continue
                keep = rows > o + 1
                k0, k1 = jnp.where(keep, k0, 0.0), jnp.where(keep, k1, 0.0)
            left[i] = left[i] - (k0 * q0 + k1 * q1)
            right[i] = right[i] - (k0 * t0 + k1 * t1)
    return jnp.concatenate(done, axis=0)


def invert_kernel(c_ref, z_ref, m_ref, p_ref):
    n = c_ref.shape[0]
    m_ref[...] = c_ref[...]
    z_ref[...] = jnp.where(
        lax.broadcasted_iota(jnp.int32, (n, n), 0) == lax.broadcasted_iota(jnp.int32, (n, n), 1), 1.0, 0.0)

    def step(k, carry):
        here = pl.ds(pl.multiple_of(k * TILE, TILE), TILE)
        inv = factor_tile(m_ref[here, here])
        below = lax.broadcasted_iota(jnp.int32, (n, TILE), 0) >= (k + 1) * TILE
        p_ref[...] = jnp.where(below, dot_nt(m_ref[:, here], inv), 0.0)
        z_ref[here, :] = dot_nn(inv, z_ref[here, :])
        panel = p_ref[...]
        for part in range(0, n, BLOCK):
            cut = slice(part, part + BLOCK)
            m_ref[:, cut] = m_ref[:, cut] - dot_nt(panel, p_ref[cut, :])
            z_ref[:, cut] = z_ref[:, cut] - dot_nn(panel, z_ref[here, cut])
        return carry

    lax.fori_loop(0, n // TILE, step, 0)


def inverse_factor(cross):
    n = cross.shape[0]
    return pl.pallas_call(
        invert_kernel,
        out_shape=jax.ShapeDtypeStruct((n, n), jnp.float32),
        in_specs=[pl.BlockSpec(memory_space=pltpu.VMEM)],
        out_specs=pl.BlockSpec(memory_space=pltpu.VMEM),
        scratch_shapes=[pltpu.VMEM((n, n), jnp.float32), pltpu.VMEM((n, TILE), jnp.float32)],
        compiler_params=pltpu.CompilerParams(vmem_limit_bytes=32 * 1024 * 1024),
        cost_estimate=pl.CostEstimate(flops=40_000_000_000, bytes_accessed=8 * n * n, transcendentals=0),
    )(cross)


def own_rows(array, start):
    rows = array.shape[0]
    inside = jnp.clip(start, 0, rows - BLOCK)
    part = lax.dynamic_slice_in_dim(array, inside, BLOCK, 0)
    blank = jnp.zeros_like(part)
    shift = jnp.clip(start - inside, -BLOCK, BLOCK)
    return lax.dynamic_slice_in_dim(jnp.concatenate([blank, part, blank], axis=0), BLOCK + shift, BLOCK, 0)


def body(panels, weights, block_ids):
    local_rows = panels.shape[0]
    picks = block_ids.shape[0]
    cols = weights.shape[1]
    first_row = lax.axis_index("row") * local_rows
    starts = [block_ids[k] * BLOCK - first_row for k in range(picks)]

    pieces = []
    for k in range(picks):
        taken = own_rows(panels, starts[k])
        pieces += [taken[:, j * BLOCK : (j + 1) * BLOCK] for j in range(k + 1)]
    pieces = lax.psum(jnp.concatenate(pieces, axis=0), "row")
    listed = jnp.concatenate([own_rows(weights, starts[k]) for k in range(picks)], axis=0)
    listed = lax.psum(listed, "row")

    def piece(i, j):
        if i < j:
            return piece(j, i).T
        at = (i * (i + 1) // 2 + j) * BLOCK
        return pieces[at : at + BLOCK]

    cross = jnp.concatenate(
        [jnp.concatenate([piece(i, j) for j in range(picks)], axis=1) for i in range(picks)], axis=0)
    inverse = inverse_factor(cross)
    left = lax.dot_general(panels, inverse, (((1,), (1,)), ((), ())), precision=split_mode)
    middle = jnp.dot(inverse, listed, precision=split_mode)
    losses = jnp.sum((middle * middle).reshape(picks, -1), axis=1) / (BLOCK * cols * 2.0)
    local = jnp.arange(local_rows, dtype=jnp.int32)
    keep = jnp.ones((local_rows,), jnp.bool_)
    for start in starts:
        keep = keep & ((local < start) | (local >= start + BLOCK))
    update = weights - jnp.dot(left, middle, precision=split_mode)
    return (jnp.where(keep[:, None], update, 0.0), losses)


def solution(mesh):
    in_specs = (P(("groups", "row"), None), P(("groups", "row"), None), P("groups"))
    out_specs = (P(("groups", "row"), None), P("groups"))
    return jax.shard_map(body, mesh=mesh, in_specs=in_specs, out_specs=out_specs, check_vma=False)
```

```python
import functools
import math

import jax
import jax.numpy as jnp
from jax import lax
from jax.experimental import pallas as pl
from jax.experimental.pallas import tpu as pltpu
from jax.sharding import PartitionSpec as P

BLOCK = 256
TILE = 128
exact_mode = lax.Precision.HIGHEST
split_mode = lax.Precision.HIGH


def dot_nt(a, b):
    return lax.dot_general(a, b, (((1,), (1,)), ((), ())), precision=exact_mode,
                           preferred_element_type=jnp.float32)


def dot_nn(a, b):
    return lax.dot_general(a, b, (((1,), (0,)), ((), ())), precision=exact_mode,
                           preferred_element_type=jnp.float32)


def factor_tile(tile):
    n = TILE
    groups = n // 8
    rows = lax.broadcasted_iota(jnp.int32, (8, n), 0)
    lanes = lax.broadcasted_iota(jnp.int32, (8, n), 1)
    left = [tile[8 * g : 8 * g + 8, :] for g in range(groups)]
    right = [jnp.where(lanes == rows + 8 * g, 1.0, 0.0) for g in range(groups)]
    done = []
    for j in range(0, n, 2):
        g, o = j // 8, j % 8
        c0 = {i: jnp.broadcast_to(left[i][:, j : j + 1], (8, n)) for i in range(g, groups)}
        c1 = {i: jnp.broadcast_to(left[i][:, j + 1 : j + 2], (8, n)) for i in range(g, groups)}
        a = c0[g][o : o + 1]
        b = c0[g][o + 1 : o + 2]
        d = c1[g][o + 1 : o + 2]
        inv_det = 1.0 / (a * d - b * b)
        m00, m01, m11 = d * inv_det, -b * inv_det, a * inv_det
        r0, r1 = left[g][o : o + 1], left[g][o + 1 : o + 2]
        s0, s1 = right[g][o : o + 1], right[g][o + 1 : o + 2]
        q0, q1 = m00 * r0 + m01 * r1, m01 * r0 + m11 * r1
        t0, t1 = m00 * s0 + m01 * s1, m01 * s0 + m11 * s1
        ratio = b / a
        done.append(s0 * lax.rsqrt(a))
        done.append((s1 - ratio * s0) * lax.rsqrt(d - b * ratio))
        for i in range(g, groups):
            k0, k1 = c0[i], c1[i]
            if i == g:
                if o == 6:
                    continue
                keep = rows > o + 1
                k0, k1 = jnp.where(keep, k0, 0.0), jnp.where(keep, k1, 0.0)
            left[i] = left[i] - (k0 * q0 + k1 * q1)
            right[i] = right[i] - (k0 * t0 + k1 * t1)
    return jnp.concatenate(done, axis=0)


def invert_kernel(c_ref, z_ref, m_ref, p_ref):
    n = c_ref.shape[0]
    m_ref[...] = c_ref[...]
    z_ref[...] = jnp.where(
        lax.broadcasted_iota(jnp.int32, (n, n), 0) == lax.broadcasted_iota(jnp.int32, (n, n), 1), 1.0, 0.0)

    def step(k, carry):
        here = pl.ds(pl.multiple_of(k * TILE, TILE), TILE)
        inv = factor_tile(m_ref[here, here])
        below = lax.broadcasted_iota(jnp.int32, (n, TILE), 0) >= (k + 1) * TILE
        p_ref[...] = jnp.where(below, dot_nt(m_ref[:, here], inv), 0.0)
        z_ref[here, :] = dot_nn(inv, z_ref[here, :])
        panel = p_ref[...]
        for part in range(0, n, BLOCK):
            cut = slice(part, part + BLOCK)
            m_ref[:, cut] = m_ref[:, cut] - dot_nt(panel, p_ref[cut, :])
            z_ref[:, cut] = z_ref[:, cut] - dot_nn(panel, z_ref[here, cut])
        return carry

    lax.fori_loop(0, n // TILE, step, 0)


def inverse_factor(cross):
    n = cross.shape[0]
    return pl.pallas_call(
        invert_kernel,
        out_shape=jax.ShapeDtypeStruct((n, n), jnp.float32),
        in_specs=[pl.BlockSpec(memory_space=pltpu.VMEM)],
        out_specs=pl.BlockSpec(memory_space=pltpu.VMEM),
        scratch_shapes=[pltpu.VMEM((n, n), jnp.float32), pltpu.VMEM((n, TILE), jnp.float32)],
        compiler_params=pltpu.CompilerParams(vmem_limit_bytes=32 * 1024 * 1024),
        cost_estimate=pl.CostEstimate(flops=40_000_000_000, bytes_accessed=8 * n * n, transcendentals=0),
    )(cross)


def pick_kernel(picks, chunk, tri, starts_ref, x_ref, o_ref, sems):
    o_ref[...] = jnp.zeros_like(o_ref)
    rows = x_ref.shape[0]

    def each(act):
        number = 0
        for k in range(picks):
            for c in range(BLOCK // chunk):
                at = starts_ref[k] + c * chunk
                copies = []
                for j in range(k + 1 if tri else 1):
                    place = (k * (k + 1) // 2 + j if tri else k) * BLOCK + c * chunk
                    source = x_ref.at[pl.ds(pl.multiple_of(jnp.clip(at, 0, rows - chunk), 8), chunk)]
                    if tri:
                        source = source.at[:, j * BLOCK : (j + 1) * BLOCK]
                    copies.append(pltpu.make_async_copy(source, o_ref.at[pl.ds(place, chunk)], sems.at[number]))
                    number += 1

                @pl.when((at >= 0) & (at < rows))
                def _(copies=copies):
                    for copy in copies:
                        act(copy)

    each(lambda copy: copy.start())
    each(lambda copy: copy.wait())


def pick_rows(array, starts, picks, tri):
    rows, cols = array.shape
    chunk = math.gcd(BLOCK, rows)
    blocks = picks * (picks + 1) // 2 if tri else picks
    out = (blocks * BLOCK, BLOCK if tri else cols)
    return pl.pallas_call(
        functools.partial(pick_kernel, picks, chunk, tri),
        out_shape=jax.ShapeDtypeStruct(out, array.dtype),
        in_specs=[pl.BlockSpec(memory_space=pltpu.SMEM), pl.BlockSpec(memory_space=pl.ANY)],
        out_specs=pl.BlockSpec(memory_space=pltpu.VMEM),
        scratch_shapes=[pltpu.SemaphoreType.DMA((blocks * (BLOCK // chunk),))],
        compiler_params=pltpu.CompilerParams(vmem_limit_bytes=24 * 1024 * 1024),
        cost_estimate=pl.CostEstimate(flops=0, bytes_accessed=8 * out[0] * out[1], transcendentals=0),
    )(starts, array)


def sum_kernel(n, x_ref, o_ref, acc, got, full, send_sems, recv_sems):
    me = lax.axis_index("row")
    steps = n.bit_length() - 1
    rows = x_ref.shape[0]
    sides = [lax.rem(me // (1 << s), 2) for s in range(steps)]
    partners = [me + (1 << s) * (1 - 2 * sides[s]) for s in range(steps)]
    barrier = pltpu.get_barrier_semaphore()
    for partner in partners:
        pl.semaphore_signal(barrier, inc=1, device_id={"row": partner}, device_id_type=pl.DeviceIdType.MESH)
    acc[...] = x_ref[...]
    pl.semaphore_wait(barrier, steps)

    def copy(source, target, number, partner):
        return pltpu.make_async_remote_copy(
            src_ref=source, dst_ref=target, send_sem=send_sems.at[number], recv_sem=recv_sems.at[number],
            device_id={"row": partner}, device_id_type=pl.DeviceIdType.MESH)

    low, size, lows = 0, rows, []
    for s in range(steps):
        half = size // 2
        away = pl.multiple_of(low + (1 - sides[s]) * half, 8)
        low = pl.multiple_of(low + sides[s] * half, 8)
        landing = pl.ds(rows - size, half)
        sent = copy(acc.at[pl.ds(away, half)], got.at[landing], s, partners[s])
        sent.start()
        sent.wait()
        acc[pl.ds(low, half), :] = acc[pl.ds(low, half), :] + got[landing, :]
        size = half
        lows.append(low)
    full[pl.ds(low, size), :] = acc[pl.ds(low, size), :]
    for s in reversed(range(steps)):
        here = pl.ds(lows[s], size)
        sent = copy(full.at[here], full.at[here], steps + s, partners[s])
        sent.start()
        sent.wait()
        size = size * 2
    o_ref[...] = full[...]


def sum_rows(array, n):
    rows, cols = array.shape
    steps = n.bit_length() - 1
    return pl.pallas_call(
        functools.partial(sum_kernel, n),
        out_shape=jax.ShapeDtypeStruct(array.shape, array.dtype),
        in_specs=[pl.BlockSpec(memory_space=pltpu.VMEM)],
        out_specs=pl.BlockSpec(memory_space=pltpu.VMEM),
        scratch_shapes=[pltpu.VMEM((rows, cols), array.dtype)] * 3
        + [pltpu.SemaphoreType.DMA((2 * steps,)), pltpu.SemaphoreType.DMA((2 * steps,))],
        compiler_params=pltpu.CompilerParams(
            vmem_limit_bytes=24 * 1024 * 1024, collective_id=0, has_side_effects=True),
        cost_estimate=pl.CostEstimate(flops=40_000_000_000, bytes_accessed=8 * rows * cols, transcendentals=0),
    )(array)


def body(panels, weights, block_ids):
    local_rows = panels.shape[0]
    picks = block_ids.shape[0]
    cols = weights.shape[1]
    first_row = lax.axis_index("row") * local_rows
    starts = [block_ids[k] * BLOCK - first_row for k in range(picks)]

    local_starts = jnp.stack(starts)
    pieces = pick_rows(panels, local_starts, picks, True)
    listed = pick_rows(weights, local_starts, picks, False)
    pieces, listed = lax.optimization_barrier((pieces, listed))
    listed = lax.psum(listed, "row")
    pieces = sum_rows(pieces, lax.axis_size("row"))

    def piece(i, j):
        if i < j:
            return piece(j, i).T
        at = (i * (i + 1) // 2 + j) * BLOCK
        return pieces[at : at + BLOCK]

    cross = jnp.concatenate(
        [jnp.concatenate([piece(i, j) for j in range(picks)], axis=1) for i in range(picks)], axis=0)
    inverse = inverse_factor(cross)
    left = lax.dot_general(panels, inverse, (((1,), (1,)), ((), ())), precision=split_mode)
    middle = jnp.dot(inverse, listed, precision=split_mode)
    losses = jnp.sum((middle * middle).reshape(picks, -1), axis=1) / (BLOCK * cols * 2.0)
    local = jnp.arange(local_rows, dtype=jnp.int32)
    keep = jnp.ones((local_rows,), jnp.bool_)
    for start in starts:
        keep = keep & ((local < start) | (local >= start + BLOCK))
    update = weights - jnp.dot(left, middle, precision=split_mode)
    return (jnp.where(keep[:, None], update, 0.0), losses)


def solution(mesh):
    in_specs = (P(("groups", "row"), None), P(("groups", "row"), None), P("groups"))
    out_specs = (P(("groups", "row"), None), P("groups"))
    return jax.shard_map(body, mesh=mesh, in_specs=in_specs, out_specs=out_specs, check_vma=False)
```

```python
import functools
import math

import jax
import jax.numpy as jnp
from jax import lax
from jax.experimental import pallas as pl
from jax.experimental.pallas import tpu as pltpu
from jax.sharding import PartitionSpec as P

BLOCK = 256
TILE = 128
exact_mode = lax.Precision.HIGHEST
split_mode = lax.Precision.HIGH


def dot_nt(a, b):
    return lax.dot_general(a, b, (((1,), (1,)), ((), ())), precision=exact_mode,
                           preferred_element_type=jnp.float32)


def dot_nn(a, b):
    return lax.dot_general(a, b, (((1,), (0,)), ((), ())), precision=exact_mode,
                           preferred_element_type=jnp.float32)


def factor_tile(tile):
    n = TILE
    groups = n // 8
    rows = lax.broadcasted_iota(jnp.int32, (8, n), 0)
    lanes = lax.broadcasted_iota(jnp.int32, (8, n), 1)
    left = [tile[8 * g : 8 * g + 8, :] for g in range(groups)]
    right = [jnp.where(lanes == rows + 8 * g, 1.0, 0.0) for g in range(groups)]
    done = []
    for j in range(0, n, 2):
        g, o = j // 8, j % 8
        c0 = {i: jnp.broadcast_to(left[i][:, j : j + 1], (8, n)) for i in range(g, groups)}
        c1 = {i: jnp.broadcast_to(left[i][:, j + 1 : j + 2], (8, n)) for i in range(g, groups)}
        a = c0[g][o : o + 1]
        b = c0[g][o + 1 : o + 2]
        d = c1[g][o + 1 : o + 2]
        inv_det = 1.0 / (a * d - b * b)
        m00, m01, m11 = d * inv_det, -b * inv_det, a * inv_det
        r0, r1 = left[g][o : o + 1], left[g][o + 1 : o + 2]
        s0, s1 = right[g][o : o + 1], right[g][o + 1 : o + 2]
        q0, q1 = m00 * r0 + m01 * r1, m01 * r0 + m11 * r1
        t0, t1 = m00 * s0 + m01 * s1, m01 * s0 + m11 * s1
        ratio = b / a
        done.append(s0 * lax.rsqrt(a))
        done.append((s1 - ratio * s0) * lax.rsqrt(d - b * ratio))
        for i in range(g, groups):
            k0, k1 = c0[i], c1[i]
            if i == g:
                if o == 6:
                    continue
                keep = rows > o + 1
                k0, k1 = jnp.where(keep, k0, 0.0), jnp.where(keep, k1, 0.0)
            left[i] = left[i] - (k0 * q0 + k1 * q1)
            right[i] = right[i] - (k0 * t0 + k1 * t1)
    return jnp.concatenate(done, axis=0)


def invert_kernel(c_ref, z_ref, m_ref, p_ref):
    n = c_ref.shape[0]
    m_ref[...] = c_ref[...]
    z_ref[...] = jnp.where(
        lax.broadcasted_iota(jnp.int32, (n, n), 0) == lax.broadcasted_iota(jnp.int32, (n, n), 1), 1.0, 0.0)

    def step(k, carry):
        here = pl.ds(pl.multiple_of(k * TILE, TILE), TILE)
        inv = factor_tile(m_ref[here, here])
        below = lax.broadcasted_iota(jnp.int32, (n, TILE), 0) >= (k + 1) * TILE
        p_ref[...] = jnp.where(below, dot_nt(m_ref[:, here], inv), 0.0)
        z_ref[here, :] = dot_nn(inv, z_ref[here, :])
        panel = p_ref[...]
        for part in range(0, n, BLOCK):
            cut = slice(part, part + BLOCK)
            last = k == n // TILE - 1

            @pl.when(jnp.logical_not(last) & (part + BLOCK > (k + 1) * TILE))
            def _(cut=cut):
                m_ref[:, cut] = m_ref[:, cut] - dot_nt(panel, p_ref[cut, :])

            @pl.when(jnp.logical_not(last) & (part <= k * TILE))
            def _(cut=cut):
                z_ref[:, cut] = z_ref[:, cut] - dot_nn(panel, z_ref[here, cut])

        return carry

    lax.fori_loop(0, n // TILE, step, 0)


def inverse_factor(cross):
    n = cross.shape[0]
    return pl.pallas_call(
        invert_kernel,
        out_shape=jax.ShapeDtypeStruct((n, n), jnp.float32),
        in_specs=[pl.BlockSpec(memory_space=pltpu.VMEM)],
        out_specs=pl.BlockSpec(memory_space=pltpu.VMEM),
        scratch_shapes=[pltpu.VMEM((n, n), jnp.float32), pltpu.VMEM((n, TILE), jnp.float32)],
        compiler_params=pltpu.CompilerParams(vmem_limit_bytes=32 * 1024 * 1024),
        cost_estimate=pl.CostEstimate(flops=40_000_000_000, bytes_accessed=8 * n * n, transcendentals=0),
    )(cross)


def pick_kernel(picks, chunk, tri, starts_ref, x_ref, o_ref, sems):
    o_ref[...] = jnp.zeros_like(o_ref)
    rows = x_ref.shape[0]

    def each(act):
        number = 0
        for k in range(picks):
            for c in range(BLOCK // chunk):
                at = starts_ref[k] + c * chunk
                copies = []
                for j in range(k + 1 if tri else 1):
                    place = (k * (k + 1) // 2 + j if tri else k) * BLOCK + c * chunk
                    source = x_ref.at[pl.ds(pl.multiple_of(jnp.clip(at, 0, rows - chunk), 8), chunk)]
                    if tri:
                        source = source.at[:, j * BLOCK : (j + 1) * BLOCK]
                    copies.append(pltpu.make_async_copy(source, o_ref.at[pl.ds(place, chunk)], sems.at[number]))
                    number += 1

                @pl.when((at >= 0) & (at < rows))
                def _(copies=copies):
                    for copy in copies:
                        act(copy)

    each(lambda copy: copy.start())
    each(lambda copy: copy.wait())


def pick_rows(array, starts, picks, tri):
    rows, cols = array.shape
    chunk = math.gcd(BLOCK, rows)
    blocks = picks * (picks + 1) // 2 if tri else picks
    out = (blocks * BLOCK, BLOCK if tri else cols)
    return pl.pallas_call(
        functools.partial(pick_kernel, picks, chunk, tri),
        out_shape=jax.ShapeDtypeStruct(out, array.dtype),
        in_specs=[pl.BlockSpec(memory_space=pltpu.SMEM), pl.BlockSpec(memory_space=pl.ANY)],
        out_specs=pl.BlockSpec(memory_space=pltpu.VMEM),
        scratch_shapes=[pltpu.SemaphoreType.DMA((blocks * (BLOCK // chunk),))],
        compiler_params=pltpu.CompilerParams(vmem_limit_bytes=24 * 1024 * 1024),
        cost_estimate=pl.CostEstimate(flops=0, bytes_accessed=8 * out[0] * out[1], transcendentals=0),
    )(starts, array)


def sum_kernel(n, x_ref, o_ref, acc, got, full, send_sems, recv_sems):
    me = lax.axis_index("row")
    steps = n.bit_length() - 1
    rows = x_ref.shape[0]
    sides = [lax.rem(me // (1 << s), 2) for s in range(steps)]
    partners = [me + (1 << s) * (1 - 2 * sides[s]) for s in range(steps)]
    barrier = pltpu.get_barrier_semaphore()
    for partner in partners:
        pl.semaphore_signal(barrier, inc=1, device_id={"row": partner}, device_id_type=pl.DeviceIdType.MESH)
    acc[...] = x_ref[...]
    pl.semaphore_wait(barrier, steps)

    def copy(source, target, number, partner):
        return pltpu.make_async_remote_copy(
            src_ref=source, dst_ref=target, send_sem=send_sems.at[number], recv_sem=recv_sems.at[number],
            device_id={"row": partner}, device_id_type=pl.DeviceIdType.MESH)

    low, size, lows = 0, rows, []
    for s in range(steps):
        half = size // 2
        away = pl.multiple_of(low + (1 - sides[s]) * half, 8)
        low = pl.multiple_of(low + sides[s] * half, 8)
        landing = pl.ds(rows - size, half)
        sent = copy(acc.at[pl.ds(away, half)], got.at[landing], s, partners[s])
        sent.start()
        sent.wait()
        acc[pl.ds(low, half), :] = acc[pl.ds(low, half), :] + got[landing, :]
        size = half
        lows.append(low)
    full[pl.ds(low, size), :] = acc[pl.ds(low, size), :]
    for s in reversed(range(steps)):
        here = pl.ds(lows[s], size)
        sent = copy(full.at[here], full.at[here], steps + s, partners[s])
        sent.start()
        sent.wait()
        size = size * 2
    o_ref[...] = full[...]


def sum_rows(array, n):
    rows, cols = array.shape
    steps = n.bit_length() - 1
    return pl.pallas_call(
        functools.partial(sum_kernel, n),
        out_shape=jax.ShapeDtypeStruct(array.shape, array.dtype),
        in_specs=[pl.BlockSpec(memory_space=pltpu.VMEM)],
        out_specs=pl.BlockSpec(memory_space=pltpu.VMEM),
        scratch_shapes=[pltpu.VMEM((rows, cols), array.dtype)] * 3
        + [pltpu.SemaphoreType.DMA((2 * steps,)), pltpu.SemaphoreType.DMA((2 * steps,))],
        compiler_params=pltpu.CompilerParams(
            vmem_limit_bytes=24 * 1024 * 1024, collective_id=0, has_side_effects=True),
        cost_estimate=pl.CostEstimate(flops=40_000_000_000, bytes_accessed=8 * rows * cols, transcendentals=0),
    )(array)


def body(panels, weights, block_ids):
    local_rows = panels.shape[0]
    picks = block_ids.shape[0]
    cols = weights.shape[1]
    first_row = lax.axis_index("row") * local_rows
    starts = [block_ids[k] * BLOCK - first_row for k in range(picks)]

    local_starts = jnp.stack(starts)
    pieces = pick_rows(panels, local_starts, picks, True)
    listed = pick_rows(weights, local_starts, picks, False)
    pieces, listed = lax.optimization_barrier((pieces, listed))
    listed = lax.psum(listed, "row")
    pieces = sum_rows(pieces, lax.axis_size("row"))

    def piece(i, j):
        if i < j:
            return piece(j, i).T
        at = (i * (i + 1) // 2 + j) * BLOCK
        return pieces[at : at + BLOCK]

    cross = jnp.concatenate(
        [jnp.concatenate([piece(i, j) for j in range(picks)], axis=1) for i in range(picks)], axis=0)
    inverse = inverse_factor(cross)
    left = lax.dot_general(panels, inverse, (((1,), (1,)), ((), ())), precision=split_mode)
    middle = jnp.dot(inverse, listed, precision=split_mode)
    losses = jnp.sum((middle * middle).reshape(picks, -1), axis=1) / (BLOCK * cols * 2.0)
    local = jnp.arange(local_rows, dtype=jnp.int32)
    keep = jnp.ones((local_rows,), jnp.bool_)
    for start in starts:
        keep = keep & ((local < start) | (local >= start + BLOCK))
    update = weights - jnp.dot(left, middle, precision=split_mode)
    return (jnp.where(keep[:, None], update, 0.0), losses)


def solution(mesh):
    in_specs = (P(("groups", "row"), None), P(("groups", "row"), None), P("groups"))
    out_specs = (P(("groups", "row"), None), P("groups"))
    return jax.shard_map(body, mesh=mesh, in_specs=in_specs, out_specs=out_specs, check_vma=False)
```
